32 devices in a mesh: dp: 4 (over z), context: 8 (over y, x, core).
Axes of the slice: x: 2, y: 2, z: 4, core: 2. Of those that a mesh axis runs over, the one named last changes fastest.
Arguments:
- query_in: bfloat16 [4, 4096, 1024], P('dp', 'context'), may hold values from -6 to 6
- key_in: bfloat16 [4, 4096, 1024], P('dp', 'context'), may hold values from -6 to 6
- value_in: bfloat16 [4, 4096, 1024], P('dp', 'context'), may hold values from -6 to 6
- out_grad: bfloat16 [4, 4096, 2048], P('dp', 'context'), may hold values from -6 to 6
- out_weight: bfloat16 [1024, 2048], P('context'), may hold values from -0.1875 to 0.1875
Outputs:
- output: bfloat16 [4, 4096, 2048], P('dp', 'context')
- query_grad: bfloat16 [4, 4096, 1024], P('dp', 'context')
- key_grad: bfloat16 [4, 4096, 1024], P('dp', 'context')
- value_grad: bfloat16 [4, 4096, 1024], P('dp', 'context')
- weight_grad: float32 [1024, 2048], P('context')
The draws below stay inside these ranges and needn't reach their ends.
All inputs are finite; a program needn't handle non-finite values.
Results may differ from the reference program's by a relative error of at most 0.025.
Values may be sent and summed in bfloat16 or wider, within the bound.
A program may use at most 192 MiB of HBM per device.

```python
import math
import jax
import jax.numpy as jnp
from jax import lax

HEADS = 8
HEAD_DIM = 128
D = 2048
TOK_DEV = 512
HD = 1024
LENGTH = 4096
SEQS = 4


def steps_of(own_key, shape, shards, least, high):
    def one(position, shards_of):
        steps = jax.random.uniform(jax.random.fold_in(jax.random.fold_in(own_key, 6), position), (shards_of,), jnp.float32, least / len(shards), high / len(shards))
        return jnp.repeat(jnp.exp(steps), shape[position] // shards_of).reshape((-1,) + (1,) * (len(shape) - position - 1))

    gain = one(*shards[0])
    for cut in shards[1:]:
        gain = gain * one(*cut)
    return gain


def centred(own_key, shape, deviation, reach, split=(), held_as=jnp.bfloat16):
    factor_of = steps_of(own_key, shape, split, -0.22, 0.18) if split else 1.0
    entries = jax.random.normal(own_key, shape, jnp.float32) * deviation * factor_of
    return jnp.minimum(jnp.maximum(entries, -reach), reach).astype(held_as)


def setup_inputs(seed: int = 0) -> dict:
    splits = jax.random.split(jax.random.key(seed), 6)
    return {
        "query_in": centred(splits[0], (SEQS, LENGTH, HD), 1.0, 6.0, ((0, 4), (1, 8))),
        "key_in": centred(splits[1], (SEQS, LENGTH, HD), 1.0, 6.0, ((0, 4), (1, 8))),
        "value_in": centred(splits[2], (SEQS, LENGTH, HD), 1.0, 6.0, ((0, 4), (1, 8))),
        "out_grad": centred(splits[3], (SEQS, LENGTH, D), 1.0, 6.0, ((0, 4), (1, 8))),
        "out_weight": centred(splits[4], (HD, D), HD ** -0.5, 0.1875, ((0, 8),)),
    }


def to_blocks(array, seq_count, blocks):
    return array.reshape(seq_count * blocks, TOK_DEV, HEADS, HEAD_DIM)

def block_states(pieces):
    query_part, key_part, value_part, grad_part = pieces
    kv_part = jnp.einsum('shd,she->hde', key_part.astype(jnp.float32), value_part.astype(jnp.float32))
    qg_part = jnp.einsum('thd,the->hde', query_part.astype(jnp.float32), grad_part.astype(jnp.float32))
    return (kv_part, qg_part)

def reference(query_in, key_in, value_in, out_grad, out_weight):
    seq_count = query_in.shape[0]
    length = query_in.shape[1]
    head_width = query_in.shape[2]
    blocks = length // TOK_DEV
    att_scale = 1.0 / math.sqrt(HEAD_DIM * length)
    grad_scale = 1.0 / math.sqrt(seq_count * length)
    grad_flat = out_grad.reshape(seq_count * length, D)
    head_grad = jnp.dot(grad_flat, out_weight.T, preferred_element_type=jnp.float32).astype(jnp.bfloat16)
    query_blk = to_blocks(query_in, seq_count, blocks)
    key_blk = to_blocks(key_in, seq_count, blocks)
    value_blk = to_blocks(value_in, seq_count, blocks)
    grad_blk = to_blocks(head_grad, seq_count, blocks)
    kv_block, qg_block = lax.map(block_states, (query_blk, key_blk, value_blk, grad_blk))
    state_shape = (seq_count, blocks, HEADS, HEAD_DIM, HEAD_DIM)
    kv_block = kv_block.reshape(state_shape)
    qg_block = qg_block.reshape(state_shape)
    kv_incl = jnp.cumsum(kv_block, axis=1)
    kv_before = jnp.concatenate([jnp.zeros_like(kv_incl[:, :1]), kv_incl[:, :-1]], axis=1).astype(jnp.bfloat16)
    qg_incl = jnp.flip(jnp.cumsum(jnp.flip(qg_block, 1), axis=1), 1)
    qg_after = jnp.concatenate([qg_incl[:, 1:], jnp.zeros_like(qg_incl[:, :1])], axis=1).astype(jnp.bfloat16)
    kv_before = kv_before.reshape(seq_count * blocks, HEADS, HEAD_DIM, HEAD_DIM)
    qg_after = qg_after.reshape(seq_count * blocks, HEADS, HEAD_DIM, HEAD_DIM)
    positions = lax.broadcasted_iota(jnp.int32, (TOK_DEV, TOK_DEV), 0)
    sources = lax.broadcasted_iota(jnp.int32, (TOK_DEV, TOK_DEV), 1)
    causal = (positions >= sources)[None]

    def one_block(pieces):
        query_part, key_part, value_part, grad_part, kv_part, qg_part = pieces
        query_wide = query_part.astype(jnp.float32)
        key_wide = key_part.astype(jnp.float32)
        value_wide = value_part.astype(jnp.float32)
        grad_wide = grad_part.astype(jnp.float32)
        kv_wide = kv_part.astype(jnp.float32)
        qg_wide = qg_part.astype(jnp.float32)
        scores = jnp.einsum('thd,shd->hts', query_wide, key_wide) * att_scale
        scores = jnp.where(causal, scores, 0.0).astype(jnp.bfloat16).astype(jnp.float32)
        attended = jnp.einsum('hts,shd->thd', scores, value_wide) + att_scale * jnp.einsum('thd,hde->the', query_wide, kv_wide)
        back_scores = jnp.einsum('the,she->hts', grad_wide, value_wide) * att_scale
        back_scores = jnp.where(causal, back_scores, 0.0).astype(jnp.bfloat16).astype(jnp.float32)
        query_grad = jnp.einsum('hts,shd->thd', back_scores, key_wide) + att_scale * jnp.einsum('the,hde->thd', grad_wide, kv_wide)
        key_grad = jnp.einsum('hts,thd->shd', back_scores, query_wide) + att_scale * jnp.einsum('she,hde->shd', value_wide, qg_wide)
        value_grad = jnp.einsum('hts,the->she', scores, grad_wide) + att_scale * jnp.einsum('shd,hde->she', key_wide, qg_wide)
        return (attended.astype(jnp.bfloat16), query_grad.astype(jnp.bfloat16), key_grad.astype(jnp.bfloat16), value_grad.astype(jnp.bfloat16))
    attended, query_grad, key_grad, value_grad = lax.map(one_block, (query_blk, key_blk, value_blk, grad_blk, kv_before, qg_after))
    out_shape = (seq_count, length, head_width)
    attended_flat = attended.reshape(seq_count * length, head_width)
    output = jnp.dot(attended_flat, out_weight, preferred_element_type=jnp.float32).astype(jnp.bfloat16)
    weight_grad = jnp.dot(attended_flat.T, grad_flat, preferred_element_type=jnp.float32) * grad_scale
    return (output.reshape(seq_count, length, D), query_grad.reshape(out_shape), key_grad.reshape(out_shape), value_grad.reshape(out_shape), weight_grad)
```

```python
import functools
import math

import jax
import jax.numpy as jnp
from jax import lax
from jax.experimental import pallas as pl
from jax.experimental.pallas import tpu as pltpu
from jax.sharding import PartitionSpec as P

HEADS = 8
HEAD_DIM = 128
F32 = jnp.float32
BF16 = jnp.bfloat16


def dot_nn(a, b):
    return lax.dot_general(a, b, (((1,), (0,)), ((), ())), preferred_element_type=F32)


def dot_nt(a, b):
    return lax.dot_general(a, b, (((1,), (1,)), ((), ())), preferred_element_type=F32)


def dot_tn(a, b):
    return lax.dot_general(a, b, (((0,), (0,)), ((), ())), preferred_element_type=F32)


def loop(count, body):
    lax.fori_loop(0, count, lambda i, _: (body(i), 0)[1], 0)


def kernel(
    n, g, q_ref, k_ref, v_ref, og_ref, w_ref, out_ref, qgrad_ref, kgrad_ref, vgrad_ref, wgrad_ref,
    wfull, kv_send, kv_recv, kv_pref, kvb, qg_send, qg_recv, qg_pref, qga,
    scores, intra, att, att_t, hg, wchunk, keep, sib_send, sib_recv, x_send, x_recv,
    z_send, z_recv, z2_send, z2_recv,
    s_kv1, r_kv1, s_kv2, r_kv2, s_qg1, r_qg1, s_qg2, r_qg2,
    s_w, s_wf, r_w, s_sib, r_sib, s_x, r_x, s_z, r_z, s_z2, r_z2,
):
    me, z = lax.axis_index("context"), lax.axis_index("dp")
    nc = n // 2
    chip, core = me // 2, lax.rem(me, 2)
    sibling = chip * 2 + 1 - core
    tok, width = q_ref.shape
    model = og_ref.shape[1]
    rows = width // n
    cols = model // g
    att_scale = 1.0 / math.sqrt(HEAD_DIM * tok * n)
    grad_scale = 1.0 / math.sqrt(tok * n * g)

    def head(h):
        return pl.ds(pl.multiple_of(h * HEAD_DIM, HEAD_DIM), HEAD_DIM)

    def part(d):
        return pl.ds(pl.multiple_of(d * rows, rows), rows)

    def column(q):
        return pl.ds(pl.multiple_of(q * cols, cols), cols)

    def to(src, dst, ssem, rsem, device):
        return pltpu.make_async_remote_copy(
            src_ref=src, dst_ref=dst, send_sem=ssem, recv_sem=rsem,
            device_id=(z, device), device_id_type=pl.DeviceIdType.MESH,
        )

    def to_z(src, dst, ssem, rsem, group):
        return pltpu.make_async_remote_copy(
            src_ref=src, dst_ref=dst, send_sem=ssem, recv_sem=rsem,
            device_id=(group, me), device_id_type=pl.DeviceIdType.MESH,
        )

    barrier = pltpu.get_barrier_semaphore()

    def greet(o):
        pl.semaphore_signal(
            barrier, inc=1, device_id=(z, lax.rem(me + o + 1, n)),
            device_id_type=pl.DeviceIdType.MESH,
        )

    def greet_z(o):
        pl.semaphore_signal(
            barrier, inc=1, device_id=(lax.rem(z + o + 1, g), me),
            device_id_type=pl.DeviceIdType.MESH,
        )

    loop(n - 1, greet)
    loop(g - 1, greet_z)

    def kv_head(h):
        kv_send[head(h), :] = dot_tn(k_ref[:, head(h)], v_ref[:, head(h)]).astype(BF16)

    loop(HEADS, kv_head)
    pl.semaphore_wait(barrier, n - 1 + g - 1)

    def spread(send, recv, ssem, rsem):
        def one(o):
            d = lax.rem(me + o + 1, n)
            to(send.at[part(d)], recv.at[me], ssem.at[d], rsem.at[me], d).start()

        loop(n - 1, one)
        recv[me] = send[part(me), :]

    def arrived(send, recv, ssem, rsem):
        def one(o):
            d = lax.rem(me + o + 1, n)
            to(send.at[part(d)], recv.at[d], ssem.at[d], rsem.at[d], d).wait()

        loop(n - 1, one)

    def sums(recv, pref, backward):
        def one(i, total):
            j = n - 1 - i if backward else i
            pref[j] = total.astype(BF16)
            return total + recv[j].astype(F32)

        lax.fori_loop(0, n, one, jnp.zeros((rows, HEAD_DIM), F32))

    def give_back(pref, dst, ssem, rsem):
        def one(o):
            d = lax.rem(me + o + 1, n)
            to(pref.at[d], dst.at[part(me)], ssem.at[d], rsem.at[me], d).start()

        loop(n - 1, one)
        dst[part(me), :] = pref[me]

    def given(pref, dst, ssem, rsem):
        def one(o):
            d = lax.rem(me + o + 1, n)
            to(pref.at[d], dst.at[part(d)], ssem.at[d], rsem.at[d], d).wait()

        loop(n - 1, one)

    spread(kv_send, kv_recv, s_kv1, r_kv1)

    def own_rows(c, device):
        return to(w_ref, wfull.at[part(me)], s_w.at[c], r_w.at[me], device)

    def send_rows(o):
        c = lax.rem(chip + o + 1, nc)
        own_rows(c, c * 2 + core).start()

    loop(nc - 1, send_rows)
    own_rows(chip, sibling).start()
    wfull[part(me), :] = w_ref[...]

    causal = lax.broadcasted_iota(jnp.int32, (tok, tok), 0) >= lax.broadcasted_iota(
        jnp.int32, (tok, tok), 1
    )

    def score_head(h):
        s = dot_nt(q_ref[:, head(h)], k_ref[:, head(h)]) * att_scale
        s = jnp.where(causal, s, 0.0).astype(BF16)
        scores[h] = s
        intra[:, head(h)] = dot_nn(s, v_ref[:, head(h)])

    loop(HEADS // 2, score_head)
    arrived(kv_send, kv_recv, s_kv1, r_kv1)
    sums(kv_recv, kv_pref, False)
    give_back(kv_pref, kvb, s_kv2, r_kv2)
    loop(HEADS // 2, lambda h: score_head(h + HEADS // 2))
    given(kv_pref, kvb, s_kv2, r_kv2)

    def attend_head(h):
        a = intra[:, head(h)] + att_scale * dot_nn(q_ref[:, head(h)], kvb[head(h), :])
        a = a.astype(BF16)
        att[:, head(h)] = a
        att_t[head(h), :] = a.T

    loop(HEADS, attend_head)

    def sib_copy(i):
        return to(sib_send.at[i], sib_recv.at[i], s_sib.at[i], r_sib.at[i], sibling)

    def chunk(i):
        q = lax.rem(z + 1 + i, g)
        wchunk[...] = dot_nn(att_t[...], og_ref[:, column(q)]) * grad_scale

        def split(c):
            keep[i, c] = wchunk[part(c * 2 + core), :]
            sib_send[i, c] = wchunk[part(c * 2 + 1 - core), :].astype(BF16)

        loop(nc, split)
        sib_copy(i).start()

    loop(g, chunk)

    def row_copy(c):
        return to(
            wfull.at[part(c * 2 + core)], wfull.at[part(c * 2 + core)],
            s_wf.at[c], r_w.at[c * 2 + core], sibling,
        )

    def hand_on(o):
        c = lax.rem(chip + o + 1, nc)
        d = c * 2 + core
        to(w_ref, wfull.at[part(d)], s_w.at[c], r_w.at[d], d).wait()
        row_copy(c).start()

    def x_copy(i, c, slot):
        return to(x_send.at[i, c], x_recv.at[i, slot], s_x.at[i, c], r_x.at[i, slot], c * 2 + core)

    def cross(i):
        sib_copy(i).wait()

        def one(o):
            c = lax.rem(chip + o + 1, nc)
            x_send[i, c] = (keep[i, c] + sib_recv[i, c].astype(F32)).astype(BF16)
            x_copy(i, c, chip).start()

        loop(nc - 1, one)
        keep[i, chip] = keep[i, chip] + sib_recv[i, chip].astype(F32)

    loop(g, cross)
    loop(nc - 1, hand_on)

    own_rows(chip, sibling).wait_send()
    to(w_ref, wfull.at[part(sibling)], s_w.at[chip], r_w.at[sibling], sibling).wait_recv()

    def handed(o):
        c = lax.rem(chip + o + 1, nc)
        d = c * 2 + 1 - core
        row_copy(c).wait_send()
        to(wfull.at[part(d)], wfull.at[part(d)], s_wf.at[c], r_w.at[d], sibling).wait_recv()

    loop(nc - 1, handed)

    def grad_pair(p):
        two = pl.ds(pl.multiple_of(p * 2 * HEAD_DIM, 2 * HEAD_DIM), 2 * HEAD_DIM)
        hg[:, two] = dot_nt(og_ref[...], wfull[two, :]).astype(BF16)

    loop(HEADS // 2, grad_pair)

    def qg_head(h):
        qg_send[head(h), :] = dot_tn(q_ref[:, head(h)], hg[:, head(h)]).astype(BF16)

    loop(HEADS, qg_head)
    spread(qg_send, qg_recv, s_qg1, r_qg1)

    def z_copy(i, group, slot):
        return to_z(z_send.at[i], z_recv.at[slot], s_z.at[i], r_z.at[slot], group)

    def collect(i):
        def one(o, total):
            c = lax.rem(chip + o + 1, nc)
            x_copy(i, c, c).wait()
            return total + x_recv[i, c].astype(F32)

        return lax.fori_loop(0, nc - 1, one, keep[i, chip])

    def to_owner(i):
        z_send[i] = collect(i).astype(BF16)
        z_copy(i, lax.rem(z + 1 + i, g), z).start()

    def back_head(h):
        hgh = hg[:, head(h)]
        b = dot_nt(hgh, v_ref[:, head(h)]) * att_scale
        b = jnp.where(causal, b, 0.0).astype(BF16)
        qgrad_ref[:, head(h)] = (
            dot_nn(b, k_ref[:, head(h)]) + att_scale * dot_nt(hgh, kvb[head(h), :])
        ).astype(BF16)
        intra[:, head(h)] = dot_tn(b, q_ref[:, head(h)])

    loop(HEADS, back_head)
    arrived(qg_send, qg_recv, s_qg1, r_qg1)
    sums(qg_recv, qg_pref, True)
    give_back(qg_pref, qga, s_qg2, r_qg2)

    loop(g - 1, to_owner)

    def output_pair(p):
        wide = pl.ds(pl.multiple_of(p * 512, 512), 512)
        out_ref[:, wide] = dot_nn(att[...], wfull[:, wide]).astype(BF16)

    loop(model // 512, output_pair)
    given(qg_pref, qga, s_qg2, r_qg2)

    def last_head(h):
        qgh = qga[head(h), :]
        kgrad_ref[:, head(h)] = (
            intra[:, head(h)] + att_scale * dot_nt(v_ref[:, head(h)], qgh)
        ).astype(BF16)
        vgrad_ref[:, head(h)] = (
            dot_tn(scores[h], hg[:, head(h)]) + att_scale * dot_nn(k_ref[:, head(h)], qgh)
        ).astype(BF16)

    loop(HEADS, last_head)

    def own_total(o, total):
        s = lax.rem(z + o + 1, g)
        z_copy(0, s, s).wait_recv()
        return total + z_recv[s].astype(F32)

    final = lax.fori_loop(0, g - 1, own_total, collect(g - 1)).astype(BF16)
    z2_send[...] = final

    def z2_copy(group, slot):
        return to_z(z2_send, z2_recv.at[slot], s_z2.at[group], r_z2.at[slot], group)

    loop(g - 1, lambda o: z2_copy(lax.rem(z + o + 1, g), z).start())
    wgrad_ref[:, column(z)] = final.astype(F32)

    def finish(o):
        s = lax.rem(z + o + 1, g)
        z_copy(o, s, z).wait_send()
        z2_copy(s, s).wait()
        wgrad_ref[:, column(s)] = z2_recv[s].astype(F32)

    loop(g - 1, finish)


def on_device(query_in, key_in, value_in, out_grad, out_weight):
    n, g = lax.axis_size("context"), lax.axis_size("dp")
    tok, width = query_in.shape[1:]
    model = out_grad.shape[2]
    rows, cols, nc = width // n, model // g, n // 2
    vmem, dma = pltpu.VMEM, pltpu.SemaphoreType.DMA
    state = [
        vmem((width, HEAD_DIM), BF16), vmem((n, rows, HEAD_DIM), BF16),
        vmem((n, rows, HEAD_DIM), BF16), vmem((width, HEAD_DIM), BF16),
    ]
    scratch = [
        vmem((width, model), BF16), *state, *state,
        vmem((HEADS, tok, tok), BF16), vmem((tok, width), F32), vmem((tok, width), BF16),
        vmem((width, tok), BF16), vmem((tok, width), BF16), vmem((width, cols), F32),
        vmem((g, nc, rows, cols), F32),
        *[vmem((g, nc, rows, cols), BF16)] * 4,
        vmem((g, rows, cols), BF16), vmem((g, rows, cols), BF16),
        vmem((rows, cols), BF16), vmem((g, rows, cols), BF16),
        *[dma((n,))] * 8,
        dma((nc,)), dma((nc,)), dma((n,)), dma((g,)), dma((g,)), dma((g, nc)), dma((g, nc)),
        dma((g,)), dma((g,)), dma((g,)), dma((g,)),
    ]
    whole = pl.BlockSpec(memory_space=pltpu.VMEM)
    grads = jax.ShapeDtypeStruct((tok, width), BF16)
    outs = pl.pallas_call(
        functools.partial(kernel, n, g),
        out_shape=(
            jax.ShapeDtypeStruct((tok, model), BF16), grads, grads, grads,
            jax.ShapeDtypeStruct((rows, model), F32),
        ),
        in_specs=[whole] * 5,
        out_specs=(whole,) * 5,
        scratch_shapes=scratch,
        compiler_params=pltpu.CompilerParams(
            collective_id=0, has_side_effects=True, vmem_limit_bytes=58 * 2**20
        ),
        name="layer",
    )(query_in[0], key_in[0], value_in[0], out_grad[0], out_weight)
    return tuple(o[None] for o in outs[:4]) + (outs[4],)


def solution(mesh):
    split = P("dp", "context", None)
    rows = P("context", None)
    return jax.shard_map(
        on_device,
        mesh=mesh,
        in_specs=(split,) * 4 + (rows,),
        out_specs=(split,) * 4 + (rows,),
        check_vma=False,
    )
```

```python
import functools
import math

import jax
import jax.numpy as jnp
from jax import lax
from jax.experimental import pallas as pl
from jax.experimental.pallas import tpu as pltpu
from jax.sharding import PartitionSpec as P

HEADS = 8
HEAD_DIM = 128
F32 = jnp.float32
BF16 = jnp.bfloat16


def dot_nn(a, b):
    return lax.dot_general(a, b, (((1,), (0,)), ((), ())), preferred_element_type=F32)


def dot_nt(a, b):
    return lax.dot_general(a, b, (((1,), (1,)), ((), ())), preferred_element_type=F32)


def dot_tn(a, b):
    return lax.dot_general(a, b, (((0,), (0,)), ((), ())), preferred_element_type=F32)


def loop(count, body):
    lax.fori_loop(0, count, lambda i, _: (body(i), 0)[1], 0)


def kernel(
    n, g, q_ref, k_ref, v_ref, og_ref, w_ref, out_ref, qgrad_ref, kgrad_ref, vgrad_ref, wgrad_ref,
    wfull, kv_send, kv_recv, kv_pref, kvb, qg_send, qg_recv, qg_pref, qga,
    scores, intra, att, att_t, hg, wchunk, keep, sib_send, sib_recv, x_send, x_recv,
    z_send, z_recv, z2_send, z2_recv,
    s_kv1, r_kv1, s_kv2, r_kv2, s_qg1, r_qg1, s_qg2, r_qg2,
    s_w, s_wf, r_w, s_sib, r_sib, s_x, r_x, s_z, r_z, s_z2, r_z2,
):
    me, z = lax.axis_index("context"), lax.axis_index("dp")
    nc = n // 2
    chip, core = me // 2, lax.rem(me, 2)
    sibling = chip * 2 + 1 - core
    tok, width = q_ref.shape
    model = og_ref.shape[1]
    rows = width // n
    cols = model // g
    att_scale = 1.0 / math.sqrt(HEAD_DIM * tok * n)
    grad_scale = 1.0 / math.sqrt(tok * n * g)

    def head(h):
        return pl.ds(pl.multiple_of(h * HEAD_DIM, HEAD_DIM), HEAD_DIM)

    def part(d):
        return pl.ds(pl.multiple_of(d * rows, rows), rows)

    def column(q):
        return pl.ds(pl.multiple_of(q * cols, cols), cols)

    def to(src, dst, ssem, rsem, device):
        return pltpu.make_async_remote_copy(
            src_ref=src, dst_ref=dst, send_sem=ssem, recv_sem=rsem,
            device_id=(z, device), device_id_type=pl.DeviceIdType.MESH,
        )

    def to_z(src, dst, ssem, rsem, group):
        return pltpu.make_async_remote_copy(
            src_ref=src, dst_ref=dst, send_sem=ssem, recv_sem=rsem,
            device_id=(group, me), device_id_type=pl.DeviceIdType.MESH,
        )

    barrier = pltpu.get_barrier_semaphore()

    def greet(o):
        pl.semaphore_signal(
            barrier, inc=1, device_id=(z, lax.rem(me + o + 1, n)),
            device_id_type=pl.DeviceIdType.MESH,
        )

    def greet_z(o):
        pl.semaphore_signal(
            barrier, inc=1, device_id=(lax.rem(z + o + 1, g), me),
            device_id_type=pl.DeviceIdType.MESH,
        )

    loop(n - 1, greet)
    loop(g - 1, greet_z)

    def kv_head(h):
        kv_send[head(h), :] = dot_tn(k_ref[:, head(h)], v_ref[:, head(h)]).astype(BF16)

    loop(HEADS, kv_head)
    pl.semaphore_wait(barrier, n - 1 + g - 1)

    def spread(send, recv, ssem, rsem):
        def one(o):
            d = lax.rem(me + o + 1, n)
            to(send.at[part(d)], recv.at[me], ssem.at[d], rsem.at[me], d).start()

        loop(n - 1, one)
        recv[me] = send[part(me), :]

    def arrived(send, recv, ssem, rsem):
        def one(o):
            d = lax.rem(me + o + 1, n)
            to(send.at[part(d)], recv.at[d], ssem.at[d], rsem.at[d], d).wait()

        loop(n - 1, one)

    def sums(recv, pref, backward):
        def one(i, total):
            j = n - 1 - i if backward else i
            pref[j] = total.astype(BF16)
            return total + recv[j].astype(F32)

        lax.fori_loop(0, n, one, jnp.zeros((rows, HEAD_DIM), F32))

    def give_back(pref, dst, ssem, rsem):
        def one(o):
            d = lax.rem(me + o + 1, n)
            to(pref.at[d], dst.at[part(me)], ssem.at[d], rsem.at[me], d).start()

        loop(n - 1, one)
        dst[part(me), :] = pref[me]

    def given(pref, dst, ssem, rsem):
        def one(o):
            d = lax.rem(me + o + 1, n)
            to(pref.at[d], dst.at[part(d)], ssem.at[d], rsem.at[d], d).wait()

        loop(n - 1, one)

    spread(kv_send, kv_recv, s_kv1, r_kv1)

    def own_rows(c, device):
        return to(w_ref, wfull.at[part(me)], s_w.at[c], r_w.at[me], device)

    def send_rows(o):
        c = lax.rem(chip + o + 1, nc)
        own_rows(c, c * 2 + core).start()

    loop(nc - 1, send_rows)
    own_rows(chip, sibling).start()
    wfull[part(me), :] = w_ref[...]

    causal = lax.broadcasted_iota(jnp.int32, (tok, tok), 0) >= lax.broadcasted_iota(
        jnp.int32, (tok, tok), 1
    )

    def score_head(h):
        s = dot_nt(q_ref[:, head(h)], k_ref[:, head(h)]) * att_scale
        s = jnp.where(causal, s, 0.0).astype(BF16)
        scores[h] = s
        intra[:, head(h)] = dot_nn(s, v_ref[:, head(h)])

    loop(HEADS // 2, score_head)
    arrived(kv_send, kv_recv, s_kv1, r_kv1)
    sums(kv_recv, kv_pref, False)
    give_back(kv_pref, kvb, s_kv2, r_kv2)
    loop(HEADS // 2, lambda h: score_head(h + HEADS // 2))
    given(kv_pref, kvb, s_kv2, r_kv2)

    def attend_head(h):
        a = intra[:, head(h)] + att_scale * dot_nn(q_ref[:, head(h)], kvb[head(h), :])
        a = a.astype(BF16)
        att[:, head(h)] = a
        att_t[head(h), :] = a.T

    loop(HEADS, attend_head)

    def sib_copy(i):
        return to(sib_send.at[i], sib_recv.at[i], s_sib.at[i], r_sib.at[i], sibling)

    def chunk(i):
        q = lax.rem(z + 1 + i, g)
        wchunk[...] = dot_nn(att_t[...], og_ref[:, column(q)]) * grad_scale

        def split(c):
            keep[i, c] = wchunk[part(c * 2 + core), :]
            sib_send[i, c] = wchunk[part(c * 2 + 1 - core), :].astype(BF16)

        loop(nc, split)
        sib_copy(i).start()


    def row_copy(c):
        return to(
            wfull.at[part(c * 2 + core)], wfull.at[part(c * 2 + core)],
            s_wf.at[c], r_w.at[c * 2 + core], sibling,
        )

    def hand_on(o):
        c = lax.rem(chip + o + 1, nc)
        d = c * 2 + core
        to(w_ref, wfull.at[part(d)], s_w.at[c], r_w.at[d], d).wait()
        row_copy(c).start()

    def x_copy(i, c, slot):
        return to(x_send.at[i, c], x_recv.at[i, slot], s_x.at[i, c], r_x.at[i, slot], c * 2 + core)

    def cross(i):
        sib_copy(i).wait()

        def one(o):
            c = lax.rem(chip + o + 1, nc)
            x_send[i, c] = (keep[i, c] + sib_recv[i, c].astype(F32)).astype(BF16)
            x_copy(i, c, chip).start()

        loop(nc - 1, one)
        keep[i, chip] = keep[i, chip] + sib_recv[i, chip].astype(F32)

    chunk(0)

    def overlap(i):
        chunk(i + 1)
        cross(i)

    loop(g - 1, overlap)
    cross(g - 1)
    loop(nc - 1, hand_on)

    own_rows(chip, sibling).wait_send()
    to(w_ref, wfull.at[part(sibling)], s_w.at[chip], r_w.at[sibling], sibling).wait_recv()

    def handed(o):
        c = lax.rem(chip + o + 1, nc)
        d = c * 2 + 1 - core
        row_copy(c).wait_send()
        to(wfull.at[part(d)], wfull.at[part(d)], s_wf.at[c], r_w.at[d], sibling).wait_recv()

    loop(nc - 1, handed)

    def grad_pair(p):
        two = pl.ds(pl.multiple_of(p * 2 * HEAD_DIM, 2 * HEAD_DIM), 2 * HEAD_DIM)
        hg[:, two] = dot_nt(og_ref[...], wfull[two, :]).astype(BF16)

    loop(HEADS // 2, grad_pair)

    def qg_head(h):
        qg_send[head(h), :] = dot_tn(q_ref[:, head(h)], hg[:, head(h)]).astype(BF16)

    loop(HEADS, qg_head)
    spread(qg_send, qg_recv, s_qg1, r_qg1)

    def z_copy(i, group, slot):
        return to_z(z_send.at[i], z_recv.at[slot], s_z.at[i], r_z.at[slot], group)

    def collect(i):
        def one(o, total):
            c = lax.rem(chip + o + 1, nc)
            x_copy(i, c, c).wait()
            return total + x_recv[i, c].astype(F32)

        return lax.fori_loop(0, nc - 1, one, keep[i, chip])

    def to_owner(i):
        z_send[i] = collect(i).astype(BF16)
        z_copy(i, lax.rem(z + 1 + i, g), z).start()

    def back_head(h):
        hgh = hg[:, head(h)]
        b = dot_nt(hgh, v_ref[:, head(h)]) * att_scale
        b = jnp.where(causal, b, 0.0).astype(BF16)
        qgrad_ref[:, head(h)] = (
            dot_nn(b, k_ref[:, head(h)]) + att_scale * dot_nt(hgh, kvb[head(h), :])
        ).astype(BF16)
        intra[:, head(h)] = dot_tn(b, q_ref[:, head(h)])

    def back_some(i):
        to_owner(i)
        loop(heads_each, lambda h: back_head(i * heads_each + h))

    heads_each = HEADS // g
    loop(g - 1, back_some)
    loop(heads_each, lambda h: back_head((g - 1) * heads_each + h))

    def output_pair(p):
        wide = pl.ds(pl.multiple_of(p * 512, 512), 512)
        out_ref[:, wide] = dot_nn(att[...], wfull[:, wide]).astype(BF16)

    loop(model // 512, output_pair)
    arrived(qg_send, qg_recv, s_qg1, r_qg1)
    sums(qg_recv, qg_pref, True)
    give_back(qg_pref, qga, s_qg2, r_qg2)

    def own_total(o, total):
        s = lax.rem(z + o + 1, g)
        z_copy(0, s, s).wait_recv()
        return total + z_recv[s].astype(F32)

    final = lax.fori_loop(0, g - 1, own_total, collect(g - 1)).astype(BF16)
    z2_send[...] = final

    def z2_copy(group, slot):
        return to_z(z2_send, z2_recv.at[slot], s_z2.at[group], r_z2.at[slot], group)

    loop(g - 1, lambda o: z2_copy(lax.rem(z + o + 1, g), z).start())
    wgrad_ref[:, column(z)] = final.astype(F32)

    given(qg_pref, qga, s_qg2, r_qg2)

    def last_head(h):
        qgh = qga[head(h), :]
        kgrad_ref[:, head(h)] = (
            intra[:, head(h)] + att_scale * dot_nt(v_ref[:, head(h)], qgh)
        ).astype(BF16)
        vgrad_ref[:, head(h)] = (
            dot_tn(scores[h], hg[:, head(h)]) + att_scale * dot_nn(k_ref[:, head(h)], qgh)
        ).astype(BF16)

    loop(HEADS, last_head)

    def finish(o):
        s = lax.rem(z + o + 1, g)
        z_copy(o, s, z).wait_send()
        z2_copy(s, s).wait()
        wgrad_ref[:, column(s)] = z2_recv[s].astype(F32)

    loop(g - 1, finish)


def on_device(query_in, key_in, value_in, out_grad, out_weight):
    n, g = lax.axis_size("context"), lax.axis_size("dp")
    tok, width = query_in.shape[1:]
    model = out_grad.shape[2]
    rows, cols, nc = width // n, model // g, n // 2
    vmem, dma = pltpu.VMEM, pltpu.SemaphoreType.DMA
    state = [
        vmem((width, HEAD_DIM), BF16), vmem((n, rows, HEAD_DIM), BF16),
        vmem((n, rows, HEAD_DIM), BF16), vmem((width, HEAD_DIM), BF16),
    ]
    scratch = [
        vmem((width, model), BF16), *state, *state,
        vmem((HEADS, tok, tok), BF16), vmem((tok, width), F32), vmem((tok, width), BF16),
        vmem((width, tok), BF16), vmem((tok, width), BF16), vmem((width, cols), F32),
        vmem((g, nc, rows, cols), F32),
        *[vmem((g, nc, rows, cols), BF16)] * 4,
        vmem((g, rows, cols), BF16), vmem((g, rows, cols), BF16),
        vmem((rows, cols), BF16), vmem((g, rows, cols), BF16),
        *[dma((n,))] * 8,
        dma((nc,)), dma((nc,)), dma((n,)), dma((g,)), dma((g,)), dma((g, nc)), dma((g, nc)),
        dma((g,)), dma((g,)), dma((g,)), dma((g,)),
    ]
    whole = pl.BlockSpec(memory_space=pltpu.VMEM)
    grads = jax.ShapeDtypeStruct((tok, width), BF16)
    outs = pl.pallas_call(
        functools.partial(kernel, n, g),
        out_shape=(
            jax.ShapeDtypeStruct((tok, model), BF16), grads, grads, grads,
            jax.ShapeDtypeStruct((rows, model), F32),
        ),
        in_specs=[whole] * 5,
        out_specs=(whole,) * 5,
        scratch_shapes=scratch,
        compiler_params=pltpu.CompilerParams(
            collective_id=0, has_side_effects=True, vmem_limit_bytes=58 * 2**20
        ),
        name="layer",
    )(query_in[0], key_in[0], value_in[0], out_grad[0], out_weight)
    return tuple(o[None] for o in outs[:4]) + (outs[4],)


def solution(mesh):
    split = P("dp", "context", None)
    rows = P("context", None)
    return jax.shard_map(
        on_device,
        mesh=mesh,
        in_specs=(split,) * 4 + (rows,),
        out_specs=(split,) * 4 + (rows,),
        check_vma=False,
    )
```

```python
import functools
import math

import jax
import jax.numpy as jnp
from jax import lax
from jax.experimental import pallas as pl
from jax.experimental.pallas import tpu as pltpu
from jax.sharding import PartitionSpec as P

HEADS = 8
HEAD_DIM = 128
F32 = jnp.float32
BF16 = jnp.bfloat16


def dot_nn(a, b):
    return lax.dot_general(a, b, (((1,), (0,)), ((), ())), preferred_element_type=F32)


def dot_nt(a, b):
    return lax.dot_general(a, b, (((1,), (1,)), ((), ())), preferred_element_type=F32)


def dot_tn(a, b):
    return lax.dot_general(a, b, (((0,), (0,)), ((), ())), preferred_element_type=F32)


def loop(count, body):
    lax.fori_loop(0, count, lambda i, _: (body(i), 0)[1], 0)


def kernel(
    n, g, q_ref, k_ref, v_ref, og_ref, w_ref, out_ref, qgrad_ref, kgrad_ref, vgrad_ref, wgrad_ref,
    wfull, kv_send, kv_recv, kv_pref, kvb, qg_send, qg_recv, qg_pref, qga,
    scores, intra, att, att_t, hg, wchunk, keep, sib_send, sib_recv, x_send, x_recv,
    z_send, z_recv, z2_send, z2_recv,
    s_kv1, r_kv1, s_kv2, r_kv2, s_qg1, r_qg1, s_qg2, r_qg2,
    s_w, s_wf, r_w, s_d, r_d, s_sib, r_sib, s_x, r_x, s_z, r_z, s_z2, r_z2,
):
    me, z = lax.axis_index("context"), lax.axis_index("dp")
    nc = n // 2
    chip, core = me // 2, lax.rem(me, 2)
    sibling = chip * 2 + 1 - core
    tok, width = q_ref.shape
    model = og_ref.shape[1]
    rows = width // n
    cols = model // g
    att_scale = 1.0 / math.sqrt(HEAD_DIM * tok * n)
    grad_scale = 1.0 / math.sqrt(tok * n * g)

    def head(h):
        return pl.ds(pl.multiple_of(h * HEAD_DIM, HEAD_DIM), HEAD_DIM)

    def part(d):
        return pl.ds(pl.multiple_of(d * rows, rows), rows)

    def column(q):
        return pl.ds(pl.multiple_of(q * cols, cols), cols)

    def to(src, dst, ssem, rsem, device):
        return pltpu.make_async_remote_copy(
            src_ref=src, dst_ref=dst, send_sem=ssem, recv_sem=rsem,
            device_id=(z, device), device_id_type=pl.DeviceIdType.MESH,
        )

    def to_z(src, dst, ssem, rsem, group):
        return pltpu.make_async_remote_copy(
            src_ref=src, dst_ref=dst, send_sem=ssem, recv_sem=rsem,
            device_id=(group, me), device_id_type=pl.DeviceIdType.MESH,
        )

    barrier = pltpu.get_barrier_semaphore()

    def greet(o):
        pl.semaphore_signal(
            barrier, inc=1, device_id=(z, lax.rem(me + o + 1, n)),
            device_id_type=pl.DeviceIdType.MESH,
        )

    def greet_z(o):
        pl.semaphore_signal(
            barrier, inc=1, device_id=(lax.rem(z + o + 1, g), me),
            device_id_type=pl.DeviceIdType.MESH,
        )

    loop(n - 1, greet)
    loop(g - 1, greet_z)

    def kv_head(h):
        kv_send[head(h), :] = dot_tn(k_ref[:, head(h)], v_ref[:, head(h)]).astype(BF16)

    loop(HEADS, kv_head)
    pl.semaphore_wait(barrier, n - 1 + g - 1)

    def spread(send, recv, ssem, rsem):
        def one(o):
            d = lax.rem(me + o + 1, n)
            to(send.at[part(d)], recv.at[me], ssem.at[d], rsem.at[me], d).start()

        loop(n - 1, one)
        recv[me] = send[part(me), :]

    def arrived(send, recv, ssem, rsem):
        def one(o):
            d = lax.rem(me + o + 1, n)
            to(send.at[part(d)], recv.at[d], ssem.at[d], rsem.at[d], d).wait()

        loop(n - 1, one)

    def sums(recv, pref, backward):
        def one(i, total):
            j = n - 1 - i if backward else i
            pref[j] = total.astype(BF16)
            return total + recv[j].astype(F32)

        lax.fori_loop(0, n, one, jnp.zeros((rows, HEAD_DIM), F32))

    def give_back(pref, dst, ssem, rsem):
        def one(o):
            d = lax.rem(me + o + 1, n)
            to(pref.at[d], dst.at[part(me)], ssem.at[d], rsem.at[me], d).start()

        loop(n - 1, one)
        dst[part(me), :] = pref[me]

    def given(pref, dst, ssem, rsem):
        def one(o):
            d = lax.rem(me + o + 1, n)
            to(pref.at[d], dst.at[part(d)], ssem.at[d], rsem.at[d], d).wait()

        loop(n - 1, one)

    spread(kv_send, kv_recv, s_kv1, r_kv1)

    across = max(d for d in range(1, math.isqrt(nc) + 1) if nc % d == 0)
    down = nc // across
    cy, cx = chip // across, lax.rem(chip, across)

    def beside(o):
        return cy * across + lax.rem(cx + o + 1, across)

    def below(o):
        return lax.rem(cy + o + 1, down) * across + cx

    def corner(o, p):
        return lax.rem(cy + p + 1, down) * across + lax.rem(cx + o + 1, across)

    def own_rows(c, device):
        return to(w_ref, wfull.at[part(me)], s_w.at[c], r_w.at[me], device)

    def send_rows(c):
        own_rows(c, c * 2 + core).start()

    loop(across - 1, lambda o: send_rows(beside(o)))
    loop(down - 1, lambda p: send_rows(below(p)))
    own_rows(chip, sibling).start()
    wfull[part(me), :] = w_ref[...]

    causal = lax.broadcasted_iota(jnp.int32, (tok, tok), 0) >= lax.broadcasted_iota(
        jnp.int32, (tok, tok), 1
    )

    def score_head(h):
        s = dot_nt(q_ref[:, head(h)], k_ref[:, head(h)]) * att_scale
        s = jnp.where(causal, s, 0.0).astype(BF16)
        scores[h] = s
        intra[:, head(h)] = dot_nn(s, v_ref[:, head(h)])

    loop(HEADS // 2, score_head)
    arrived(kv_send, kv_recv, s_kv1, r_kv1)
    sums(kv_recv, kv_pref, False)
    give_back(kv_pref, kvb, s_kv2, r_kv2)
    loop(HEADS // 2, lambda h: score_head(h + HEADS // 2))
    given(kv_pref, kvb, s_kv2, r_kv2)

    def attend_head(h):
        a = intra[:, head(h)] + att_scale * dot_nn(q_ref[:, head(h)], kvb[head(h), :])
        a = a.astype(BF16)
        att[:, head(h)] = a
        att_t[head(h), :] = a.T

    loop(HEADS, attend_head)

    def sib_copy(i):
        return to(sib_send.at[i], sib_recv.at[i], s_sib.at[i], r_sib.at[i], sibling)

    def chunk(i):
        q = lax.rem(z + 1 + i, g)
        wchunk[...] = dot_nn(att_t[...], og_ref[:, column(q)]) * grad_scale

        def split(c):
            keep[i, c] = wchunk[part(c * 2 + core), :]
            sib_send[i, c] = wchunk[part(c * 2 + 1 - core), :].astype(BF16)

        loop(nc, split)
        sib_copy(i).start()


    def row_copy(c):
        return to(
            wfull.at[part(c * 2 + core)], wfull.at[part(c * 2 + core)],
            s_wf.at[c], r_w.at[c * 2 + core], sibling,
        )

    def hand_on(c):
        d = c * 2 + core
        to(w_ref, wfull.at[part(d)], s_w.at[c], r_w.at[d], d).wait()
        row_copy(c).start()

    def half_copy(half, shard, slot, device):
        piece = wfull.at[part(shard * 2 + core), pl.ds(half * (model // 2), model // 2)]
        return to(piece, piece, s_d.at[half, slot], r_d.at[half, shard], device * 2 + core)

    def pass_beside(o):
        hand_on(beside(o))
        loop(
            down - 1,
            lambda p: half_copy(0, beside(o), corner(o, p), below(p)).start(),
        )

    def pass_below(p):
        hand_on(below(p))
        loop(
            across - 1,
            lambda o: half_copy(1, below(p), corner(o, p), beside(o)).start(),
        )

    def pass_corner(o, p):
        c = corner(o, p)
        half_copy(0, c, c, below(p)).wait()
        half_copy(1, c, c, beside(o)).wait()
        row_copy(c).start()

    def x_copy(i, c, slot):
        return to(x_send.at[i, c], x_recv.at[i, slot], s_x.at[i, c], r_x.at[i, slot], c * 2 + core)

    def cross(i):
        sib_copy(i).wait()

        def one(o):
            c = lax.rem(chip + o + 1, nc)
            x_send[i, c] = (keep[i, c] + sib_recv[i, c].astype(F32)).astype(BF16)
            x_copy(i, c, chip).start()

        loop(nc - 1, one)
        keep[i, chip] = keep[i, chip] + sib_recv[i, chip].astype(F32)

    chunk(0)
    loop(across - 1, pass_beside)
    loop(down - 1, pass_below)

    def overlap(i):
        chunk(i + 1)
        cross(i)

    loop(g - 1, overlap)
    cross(g - 1)
    loop(across - 1, lambda o: loop(down - 1, lambda p: pass_corner(o, p)))

    own_rows(chip, sibling).wait_send()
    to(w_ref, wfull.at[part(sibling)], s_w.at[chip], r_w.at[sibling], sibling).wait_recv()

    def handed(o):
        c = lax.rem(chip + o + 1, nc)
        d = c * 2 + 1 - core
        row_copy(c).wait_send()
        to(wfull.at[part(d)], wfull.at[part(d)], s_wf.at[c], r_w.at[d], sibling).wait_recv()

    loop(nc - 1, handed)

    def grad_pair(p):
        two = pl.ds(pl.multiple_of(p * 2 * HEAD_DIM, 2 * HEAD_DIM), 2 * HEAD_DIM)
        hg[:, two] = dot_nt(og_ref[...], wfull[two, :]).astype(BF16)

    loop(HEADS // 2, grad_pair)

    def qg_head(h):
        qg_send[head(h), :] = dot_tn(q_ref[:, head(h)], hg[:, head(h)]).astype(BF16)

    loop(HEADS, qg_head)
    spread(qg_send, qg_recv, s_qg1, r_qg1)

    def z_copy(i, group, slot):
        return to_z(z_send.at[i], z_recv.at[slot], s_z.at[i], r_z.at[slot], group)

    def collect(i):
        def one(o, total):
            c = lax.rem(chip + o + 1, nc)
            x_copy(i, c, c).wait()
            return total + x_recv[i, c].astype(F32)

        return lax.fori_loop(0, nc - 1, one, keep[i, chip])

    def to_owner(i):
        z_send[i] = collect(i).astype(BF16)
        z_copy(i, lax.rem(z + 1 + i, g), z).start()

    def back_head(h):
        hgh = hg[:, head(h)]
        b = dot_nt(hgh, v_ref[:, head(h)]) * att_scale
        b = jnp.where(causal, b, 0.0).astype(BF16)
        qgrad_ref[:, head(h)] = (
            dot_nn(b, k_ref[:, head(h)]) + att_scale * dot_nt(hgh, kvb[head(h), :])
        ).astype(BF16)
        intra[:, head(h)] = dot_tn(b, q_ref[:, head(h)])

    def back_some(i):
        to_owner(i)
        loop(heads_each, lambda h: back_head(i * heads_each + h))

    heads_each = HEADS // g
    loop(g - 1, back_some)
    loop(heads_each, lambda h: back_head((g - 1) * heads_each + h))

    def output_pair(p):
        wide = pl.ds(pl.multiple_of(p * 512, 512), 512)
        out_ref[:, wide] = dot_nn(att[...], wfull[:, wide]).astype(BF16)

    loop(model // 512, output_pair)
    arrived(qg_send, qg_recv, s_qg1, r_qg1)
    sums(qg_recv, qg_pref, True)
    give_back(qg_pref, qga, s_qg2, r_qg2)

    def own_total(o, total):
        s = lax.rem(z + o + 1, g)
        z_copy(0, s, s).wait_recv()
        return total + z_recv[s].astype(F32)

    final = lax.fori_loop(0, g - 1, own_total, collect(g - 1)).astype(BF16)
    z2_send[...] = final

    def z2_copy(group, slot):
        return to_z(z2_send, z2_recv.at[slot], s_z2.at[group], r_z2.at[slot], group)

    loop(g - 1, lambda o: z2_copy(lax.rem(z + o + 1, g), z).start())
    wgrad_ref[:, column(z)] = final.astype(F32)

    given(qg_pref, qga, s_qg2, r_qg2)

    def last_head(h):
        qgh = qga[head(h), :]
        kgrad_ref[:, head(h)] = (
            intra[:, head(h)] + att_scale * dot_nt(v_ref[:, head(h)], qgh)
        ).astype(BF16)
        vgrad_ref[:, head(h)] = (
            dot_tn(scores[h], hg[:, head(h)]) + att_scale * dot_nn(k_ref[:, head(h)], qgh)
        ).astype(BF16)

    loop(HEADS, last_head)

    def finish(o):
        s = lax.rem(z + o + 1, g)
        z_copy(o, s, z).wait_send()
        z2_copy(s, s).wait()
        wgrad_ref[:, column(s)] = z2_recv[s].astype(F32)

    loop(g - 1, finish)


def on_device(query_in, key_in, value_in, out_grad, out_weight):
    n, g = lax.axis_size("context"), lax.axis_size("dp")
    tok, width = query_in.shape[1:]
    model = out_grad.shape[2]
    rows, cols, nc = width // n, model // g, n // 2
    vmem, dma = pltpu.VMEM, pltpu.SemaphoreType.DMA
    state = [
        vmem((width, HEAD_DIM), BF16), vmem((n, rows, HEAD_DIM), BF16),
        vmem((n, rows, HEAD_DIM), BF16), vmem((width, HEAD_DIM), BF16),
    ]
    scratch = [
        vmem((width, model), BF16), *state, *state,
        vmem((HEADS, tok, tok), BF16), vmem((tok, width), F32), vmem((tok, width), BF16),
        vmem((width, tok), BF16), vmem((tok, width), BF16), vmem((width, cols), F32),
        vmem((g, nc, rows, cols), F32),
        *[vmem((g, nc, rows, cols), BF16)] * 4,
        vmem((g, rows, cols), BF16), vmem((g, rows, cols), BF16),
        vmem((rows, cols), BF16), vmem((g, rows, cols), BF16),
        *[dma((n,))] * 8,
        dma((nc,)), dma((nc,)), dma((n,)), dma((2, nc)), dma((2, nc)), dma((g,)), dma((g,)), dma((g, nc)), dma((g, nc)),
        dma((g,)), dma((g,)), dma((g,)), dma((g,)),
    ]
    whole = pl.BlockSpec(memory_space=pltpu.VMEM)
    grads = jax.ShapeDtypeStruct((tok, width), BF16)
    outs = pl.pallas_call(
        functools.partial(kernel, n, g),
        out_shape=(
            jax.ShapeDtypeStruct((tok, model), BF16), grads, grads, grads,
            jax.ShapeDtypeStruct((rows, model), F32),
        ),
        in_specs=[whole] * 5,
        out_specs=(whole,) * 5,
        scratch_shapes=scratch,
        compiler_params=pltpu.CompilerParams(
            collective_id=0, has_side_effects=True, vmem_limit_bytes=58 * 2**20
        ),
        name="layer",
    )(query_in[0], key_in[0], value_in[0], out_grad[0], out_weight)
    return tuple(o[None] for o in outs[:4]) + (outs[4],)


def solution(mesh):
    split = P("dp", "context", None)
    rows = P("context", None)
    return jax.shard_map(
        on_device,
        mesh=mesh,
        in_specs=(split,) * 4 + (rows,),
        out_specs=(split,) * 4 + (rows,),
        check_vma=False,
    )
```

```python
import functools
import math

import jax
import jax.numpy as jnp
from jax import lax
from jax.experimental import pallas as pl
from jax.experimental.pallas import tpu as pltpu
from jax.sharding import PartitionSpec as P

HEADS = 8
HEAD_DIM = 128
F32 = jnp.float32
BF16 = jnp.bfloat16


def dot_nn(a, b):
    return lax.dot_general(a, b, (((1,), (0,)), ((), ())), preferred_element_type=F32)


def dot_nt(a, b):
    return lax.dot_general(a, b, (((1,), (1,)), ((), ())), preferred_element_type=F32)


def dot_tn(a, b):
    return lax.dot_general(a, b, (((0,), (0,)), ((), ())), preferred_element_type=F32)


def loop(count, body):
    lax.fori_loop(0, count, lambda i, _: (body(i), 0)[1], 0)


def kernel(
    n, g, q_ref, k_ref, v_ref, og_ref, w_ref, out_ref, qgrad_ref, kgrad_ref, vgrad_ref, wgrad_ref,
    wfull, kv_send, kv_recv, kv_pref, kvb, qg_send, qg_recv, qg_pref, qga,
    scores, intra, att, att_t, hg, wchunk, keep, sib_send, sib_recv, x_send, x_recv,
    z_send, z_recv, z2_send, z2_recv,
    s_kv1, r_kv1, s_kv2, r_kv2, s_qg1, r_qg1, s_qg2, r_qg2,
    s_w, s_wf, r_w, s_d, r_d, s_sib, r_sib, s_x, r_x, s_z, r_z, s_z2, r_z2,
):
    me, z = lax.axis_index("context"), lax.axis_index("dp")
    nc = n // 2
    chip, core = me // 2, lax.rem(me, 2)
    sibling = chip * 2 + 1 - core
    tok, width = q_ref.shape
    model = og_ref.shape[1]
    rows = width // n
    cols = model // g
    att_scale = 1.0 / math.sqrt(HEAD_DIM * tok * n)
    grad_scale = 1.0 / math.sqrt(tok * n * g)

    def head(h):
        return pl.ds(pl.multiple_of(h * HEAD_DIM, HEAD_DIM), HEAD_DIM)

    def part(d):
        return pl.ds(pl.multiple_of(d * rows, rows), rows)

    def column(q):
        return pl.ds(pl.multiple_of(q * cols, cols), cols)

    def to(src, dst, ssem, rsem, device):
        return pltpu.make_async_remote_copy(
            src_ref=src, dst_ref=dst, send_sem=ssem, recv_sem=rsem,
            device_id=(z, device), device_id_type=pl.DeviceIdType.MESH,
        )

    def to_z(src, dst, ssem, rsem, group):
        return pltpu.make_async_remote_copy(
            src_ref=src, dst_ref=dst, send_sem=ssem, recv_sem=rsem,
            device_id=(group, me), device_id_type=pl.DeviceIdType.MESH,
        )

    barrier = pltpu.get_barrier_semaphore()

    def greet(o):
        pl.semaphore_signal(
            barrier, inc=1, device_id=(z, lax.rem(me + o + 1, n)),
            device_id_type=pl.DeviceIdType.MESH,
        )

    def greet_z(o):
        pl.semaphore_signal(
            barrier, inc=1, device_id=(lax.rem(z + o + 1, g), me),
            device_id_type=pl.DeviceIdType.MESH,
        )

    loop(n - 1, greet)
    loop(g - 1, greet_z)

    def kv_head(h):
        kv_send[head(h), :] = dot_tn(k_ref[:, head(h)], v_ref[:, head(h)]).astype(BF16)

    loop(HEADS, kv_head)
    pl.semaphore_wait(barrier, n - 1 + g - 1)

    def spread(send, recv, ssem, rsem):
        def one(o):
            d = lax.rem(me + o + 1, n)
            to(send.at[part(d)], recv.at[me], ssem.at[d], rsem.at[me], d).start()

        loop(n - 1, one)
        recv[me] = send[part(me), :]

    def arrived(send, recv, ssem, rsem):
        def one(o):
            d = lax.rem(me + o + 1, n)
            to(send.at[part(d)], recv.at[d], ssem.at[d], rsem.at[d], d).wait()

        loop(n - 1, one)

    def sums(recv, pref, backward):
        def one(i, total):
            j = n - 1 - i if backward else i
            pref[j] = total.astype(BF16)
            return total + recv[j].astype(F32)

        lax.fori_loop(0, n, one, jnp.zeros((rows, HEAD_DIM), F32))

    def give_back(pref, dst, ssem, rsem):
        def one(o):
            d = lax.rem(me + o + 1, n)
            to(pref.at[d], dst.at[part(me)], ssem.at[d], rsem.at[me], d).start()

        loop(n - 1, one)
        dst[part(me), :] = pref[me]

    def given(pref, dst, ssem, rsem):
        def one(o):
            d = lax.rem(me + o + 1, n)
            to(pref.at[d], dst.at[part(d)], ssem.at[d], rsem.at[d], d).wait()

        loop(n - 1, one)

    spread(kv_send, kv_recv, s_kv1, r_kv1)

    across = max(d for d in range(1, math.isqrt(nc) + 1) if nc % d == 0)
    down = nc // across
    cy, cx = chip // across, lax.rem(chip, across)

    def beside(o):
        return cy * across + lax.rem(cx + o + 1, across)

    def below(o):
        return lax.rem(cy + o + 1, down) * across + cx

    def corner(o, p):
        return lax.rem(cy + p + 1, down) * across + lax.rem(cx + o + 1, across)

    def own_rows(c, device):
        return to(w_ref, wfull.at[part(me)], s_w.at[c], r_w.at[me], device)

    def send_rows(c):
        own_rows(c, c * 2 + core).start()

    loop(across - 1, lambda o: send_rows(beside(o)))
    loop(down - 1, lambda p: send_rows(below(p)))
    own_rows(chip, sibling).start()
    wfull[part(me), :] = w_ref[...]

    causal = lax.broadcasted_iota(jnp.int32, (tok, tok), 0) >= lax.broadcasted_iota(
        jnp.int32, (tok, tok), 1
    )

    def score_head(h):
        s = dot_nt(q_ref[:, head(h)], k_ref[:, head(h)]) * att_scale
        s = jnp.where(causal, s, 0.0).astype(BF16)
        scores[h] = s
        intra[:, head(h)] = dot_nn(s, v_ref[:, head(h)])

    loop(HEADS // 2, score_head)
    arrived(kv_send, kv_recv, s_kv1, r_kv1)
    sums(kv_recv, kv_pref, False)
    give_back(kv_pref, kvb, s_kv2, r_kv2)
    loop(HEADS // 2, lambda h: score_head(h + HEADS // 2))
    given(kv_pref, kvb, s_kv2, r_kv2)

    def attend_head(h):
        a = intra[:, head(h)] + att_scale * dot_nn(q_ref[:, head(h)], kvb[head(h), :])
        a = a.astype(BF16)
        att[:, head(h)] = a
        att_t[head(h), :] = a.T

    loop(HEADS, attend_head)

    def sib_copy(i):
        return to(sib_send.at[i], sib_recv.at[i], s_sib.at[i], r_sib.at[i], sibling)

    def chunk(i):
        q = lax.rem(z + 1 + i, g)
        wchunk[...] = dot_nn(att_t[...], og_ref[:, column(q)]) * grad_scale

        def split(c):
            keep[i, c] = wchunk[part(c * 2 + core), :]
            sib_send[i, c] = wchunk[part(c * 2 + 1 - core), :].astype(BF16)

        loop(nc, split)
        sib_copy(i).start()


    def row_copy(c):
        return to(
            wfull.at[part(c * 2 + core)], wfull.at[part(c * 2 + core)],
            s_wf.at[c], r_w.at[c * 2 + core], sibling,
        )

    def hand_on(c):
        d = c * 2 + core
        to(w_ref, wfull.at[part(d)], s_w.at[c], r_w.at[d], d).wait()
        row_copy(c).start()

    def half_copy(half, shard, slot, device):
        piece = wfull.at[part(shard * 2 + core), pl.ds(half * (model // 2), model // 2)]
        return to(piece, piece, s_d.at[half, slot], r_d.at[half, shard], device * 2 + core)

    def pass_beside(o):
        hand_on(beside(o))
        loop(
            down - 1,
            lambda p: half_copy(0, beside(o), corner(o, p), below(p)).start(),
        )

    def pass_below(p):
        hand_on(below(p))
        loop(
            across - 1,
            lambda o: half_copy(1, below(p), corner(o, p), beside(o)).start(),
        )

    def pass_corner(o, p):
        c = corner(o, p)
        half_copy(0, c, c, below(p)).wait()
        half_copy(1, c, c, beside(o)).wait()
        row_copy(c).start()

    def x_copy(i, c, slot):
        return to(x_send.at[i, c], x_recv.at[i, slot], s_x.at[i, c], r_x.at[i, slot], c * 2 + core)

    def cross(i):
        sib_copy(i).wait()

        def one(o):
            c = lax.rem(chip + o + 1, nc)
            x_send[i, c] = (keep[i, c] + sib_recv[i, c].astype(F32)).astype(BF16)
            x_copy(i, c, chip).start()

        loop(nc - 1, one)
        keep[i, chip] = keep[i, chip] + sib_recv[i, chip].astype(F32)

    chunk(0)
    loop(across - 1, pass_beside)
    loop(down - 1, pass_below)

    def overlap(i):
        chunk(i + 1)
        cross(i)

    loop(g - 1, overlap)
    cross(g - 1)
    loop(across - 1, lambda o: loop(down - 1, lambda p: pass_corner(o, p)))

    own_rows(chip, sibling).wait_send()
    to(w_ref, wfull.at[part(sibling)], s_w.at[chip], r_w.at[sibling], sibling).wait_recv()

    def handed(o):
        c = lax.rem(chip + o + 1, nc)
        d = c * 2 + 1 - core
        row_copy(c).wait_send()
        to(wfull.at[part(d)], wfull.at[part(d)], s_wf.at[c], r_w.at[d], sibling).wait_recv()

    loop(nc - 1, handed)

    def grad_pair(p):
        two = pl.ds(pl.multiple_of(p * 2 * HEAD_DIM, 2 * HEAD_DIM), 2 * HEAD_DIM)
        hg[:, two] = dot_nt(og_ref[...], wfull[two, :]).astype(BF16)

    loop(HEADS // 2, grad_pair)

    def qg_head(h):
        qg_send[head(h), :] = dot_tn(q_ref[:, head(h)], hg[:, head(h)]).astype(BF16)

    loop(HEADS, qg_head)
    spread(qg_send, qg_recv, s_qg1, r_qg1)

    def z_copy(i, group, slot):
        return to_z(z_send.at[i], z_recv.at[slot], s_z.at[i], r_z.at[slot], group)

    def collect(i):
        def one(o, total):
            c = lax.rem(chip + o + 1, nc)
            x_copy(i, c, c).wait()
            return total + x_recv[i, c].astype(F32)

        return lax.fori_loop(0, nc - 1, one, keep[i, chip])

    def to_owner(i):
        z_send[i] = collect(i).astype(BF16)
        z_copy(i, lax.rem(z + 1 + i, g), z).start()

    def back_head(h):
        hgh = hg[:, head(h)]
        b = dot_nt(hgh, v_ref[:, head(h)]) * att_scale
        b = jnp.where(causal, b, 0.0).astype(BF16)
        qgrad_ref[:, head(h)] = (
            dot_nn(b, k_ref[:, head(h)]) + att_scale * dot_nt(hgh, kvb[head(h), :])
        ).astype(BF16)
        intra[:, head(h)] = dot_tn(b, q_ref[:, head(h)])

    def back_some(i):
        to_owner(i)
        loop(heads_each, lambda h: back_head(i * heads_each + h))

    heads_each = HEADS // g
    loop(g - 1, back_some)
    loop(heads_each, lambda h: back_head((g - 1) * heads_each + h))

    arrived(qg_send, qg_recv, s_qg1, r_qg1)
    sums(qg_recv, qg_pref, True)
    give_back(qg_pref, qga, s_qg2, r_qg2)

    def own_total(o, total):
        s = lax.rem(z + o + 1, g)
        z_copy(0, s, s).wait_recv()
        return total + z_recv[s].astype(F32)

    final = lax.fori_loop(0, g - 1, own_total, collect(g - 1)).astype(BF16)
    z2_send[...] = final

    def z2_copy(group, slot):
        return to_z(z2_send, z2_recv.at[slot], s_z2.at[group], r_z2.at[slot], group)

    loop(g - 1, lambda o: z2_copy(lax.rem(z + o + 1, g), z).start())
    wgrad_ref[:, column(z)] = final.astype(F32)

    def output_pair(p):
        wide = pl.ds(pl.multiple_of(p * 512, 512), 512)
        out_ref[:, wide] = dot_nn(att[...], wfull[:, wide]).astype(BF16)

    loop(model // 512, output_pair)
    given(qg_pref, qga, s_qg2, r_qg2)

    def last_head(h):
        qgh = qga[head(h), :]
        kgrad_ref[:, head(h)] = (
            intra[:, head(h)] + att_scale * dot_nt(v_ref[:, head(h)], qgh)
        ).astype(BF16)
        vgrad_ref[:, head(h)] = (
            dot_tn(scores[h], hg[:, head(h)]) + att_scale * dot_nn(k_ref[:, head(h)], qgh)
        ).astype(BF16)

    loop(HEADS, last_head)

    def finish(o):
        s = lax.rem(z + o + 1, g)
        z_copy(o, s, z).wait_send()
        z2_copy(s, s).wait()
        wgrad_ref[:, column(s)] = z2_recv[s].astype(F32)

    loop(g - 1, finish)


def on_device(query_in, key_in, value_in, out_grad, out_weight):
    n, g = lax.axis_size("context"), lax.axis_size("dp")
    tok, width = query_in.shape[1:]
    model = out_grad.shape[2]
    rows, cols, nc = width // n, model // g, n // 2
    vmem, dma = pltpu.VMEM, pltpu.SemaphoreType.DMA
    state = [
        vmem((width, HEAD_DIM), BF16), vmem((n, rows, HEAD_DIM), BF16),
        vmem((n, rows, HEAD_DIM), BF16), vmem((width, HEAD_DIM), BF16),
    ]
    scratch = [
        vmem((width, model), BF16), *state, *state,
        vmem((HEADS, tok, tok), BF16), vmem((tok, width), F32), vmem((tok, width), BF16),
        vmem((width, tok), BF16), vmem((tok, width), BF16), vmem((width, cols), F32),
        vmem((g, nc, rows, cols), F32),
        *[vmem((g, nc, rows, cols), BF16)] * 4,
        vmem((g, rows, cols), BF16), vmem((g, rows, cols), BF16),
        vmem((rows, cols), BF16), vmem((g, rows, cols), BF16),
        *[dma((n,))] * 8,
        dma((nc,)), dma((nc,)), dma((n,)), dma((2, nc)), dma((2, nc)), dma((g,)), dma((g,)), dma((g, nc)), dma((g, nc)),
        dma((g,)), dma((g,)), dma((g,)), dma((g,)),
    ]
    whole = pl.BlockSpec(memory_space=pltpu.VMEM)
    grads = jax.ShapeDtypeStruct((tok, width), BF16)
    outs = pl.pallas_call(
        functools.partial(kernel, n, g),
        out_shape=(
            jax.ShapeDtypeStruct((tok, model), BF16), grads, grads, grads,
            jax.ShapeDtypeStruct((rows, model), F32),
        ),
        in_specs=[whole] * 5,
        out_specs=(whole,) * 5,
        scratch_shapes=scratch,
        compiler_params=pltpu.CompilerParams(
            collective_id=0, has_side_effects=True, vmem_limit_bytes=58 * 2**20
        ),
        name="layer",
    )(query_in[0], key_in[0], value_in[0], out_grad[0], out_weight)
    return tuple(o[None] for o in outs[:4]) + (outs[4],)


def solution(mesh):
    split = P("dp", "context", None)
    rows = P("context", None)
    return jax.shard_map(
        on_device,
        mesh=mesh,
        in_specs=(split,) * 4 + (rows,),
        out_specs=(split,) * 4 + (rows,),
        check_vma=False,
    )
```
